512 devices in a mesh: dp: 128 (over z, x, y_lo), head: 4 (over y_hi, core).
Axes of the slice: x: 4, y: 8 (y_hi: 2, y_lo: 4; y = y_hi * 4 + y_lo), z: 8, core: 2. Of those that a mesh axis runs over, the one named last changes fastest.
Arguments:
- image_features: bfloat16 [32768, 1152], P('dp', 'head'), may hold values from -6 to 6
- text_features: bfloat16 [32768, 1152], P('dp', 'head'), may hold values from -6 to 6
- image_proj: bfloat16 [1152, 1152], P('head'), may hold values from -0.1875 to 0.1875
- text_proj: bfloat16 [1152, 1152], P('head'), may hold values from -0.1875 to 0.1875
- log_scale: float32 [], replicated, may hold values from 1.5 to 2.5
- logit_bias: float32 [], replicated, may hold values from -5 to -2
Outputs:
- image_proj_grad: float32 [1152, 1152], P('head')
- text_proj_grad: float32 [1152, 1152], P('head')
The draws below stay inside these ranges and needn't reach their ends.
All inputs are finite; a program needn't handle non-finite values.
Results may differ from the reference program's by a relative error of at most 0.022.
Values may be sent and summed in bfloat16 or wider, within the bound.
No kernel may reach another device: no remote copies, remote signals or barrier semaphores. Data moves between devices by JAX's collectives and lax.ppermute only.
A program may use at most 64 MiB of HBM per device.

```python
import jax
import jax.numpy as jnp
from jax import lax

D = 1152
P_SIZE = 1152
BDEV = 256
STEPS = 8
BATCH = 32768
N_DP = 128
N_HEAD = 4


def shard_levels(own_key, shape, split, least, top_value):
    loudness, own = 1.0, jax.random.fold_in(own_key, 6)
    for dim, parts in split:
        draws = jnp.exp(jax.random.uniform(jax.random.fold_in(own, dim), (parts,), jnp.float32, least / len(split), top_value / len(split)))
        loudness = loudness * jnp.repeat(draws, shape[dim] // parts).reshape([-1 if axis == dim else 1 for axis in range(len(shape))])
    return loudness


def normal_values(stream_key, dims, width, most, pieces=(), kind=jnp.bfloat16):
    values = width * jax.random.normal(stream_key, dims, jnp.float32)
    if pieces:
        values = values * shard_levels(stream_key, dims, pieces, -0.22, 0.18)
    return jnp.clip(values, -most, most).astype(kind)


def setup_inputs(seed: int = 0) -> dict:
    key_list = jax.random.split(jax.random.key(seed), 7)
    image_features = normal_values(key_list[0], (BATCH, D), 1.0, 6.0, ((0, 128), (1, 4)))
    text_features = normal_values(key_list[1], (BATCH, D), 1.0, 6.0, ((0, 128), (1, 4)))
    image_proj = normal_values(key_list[2], (D, P_SIZE), D ** -0.5, 0.1875, ((0, 4),))
    text_proj = normal_values(key_list[3], (D, P_SIZE), D ** -0.5, 0.1875, ((0, 4),))
    log_scale = jnp.clip(jax.random.uniform(key_list[4], (), jnp.float32, 1.5, 2.5), 1.5, 2.5)
    logit_bias = jnp.clip(jax.random.uniform(key_list[5], (), jnp.float32, -5.0, -2.0), -5.0, -2.0)
    return {"image_features": image_features, "text_features": text_features, "image_proj": image_proj, "text_proj": text_proj, "log_scale": log_scale, "logit_bias": logit_bias}


epsilon = 1e-06

def normalize(raw_values):
    inverse = lax.rsqrt(lax.optimization_barrier(jnp.sum(raw_values * raw_values, axis=-1, keepdims=True)) + epsilon)
    return (raw_values * inverse, inverse)

def tangent(direction, unit_rows, inverse):
    return (direction - unit_rows * lax.optimization_barrier(jnp.sum(unit_rows * direction, axis=-1, keepdims=True))) * inverse

def project(features, weight):
    feature_width = D // N_HEAD
    summed = jnp.zeros((features.shape[0], P_SIZE), jnp.float32)
    for quarter in range(N_HEAD):
        partial_value = jnp.dot(features[:, quarter * feature_width:(quarter + 1) * feature_width], weight[quarter * feature_width:(quarter + 1) * feature_width], preferred_element_type=jnp.float32)
        partial_value = lax.optimization_barrier(partial_value.astype(jnp.bfloat16))
        summed = summed + partial_value.astype(jnp.float32)
    return summed

def reference(image_features, text_features, image_proj, text_proj, log_scale, logit_bias):
    image_unit_f, image_inverse = normalize(project(image_features, image_proj))
    text_unit_f, text_inverse = normalize(project(text_features, text_proj))
    image_units = image_unit_f.astype(jnp.bfloat16).reshape(N_DP, BDEV, P_SIZE)
    text_units = text_unit_f.astype(jnp.bfloat16).reshape(N_DP, BDEV, P_SIZE)
    logit_scale = jnp.exp(log_scale)
    quarter_rows = BDEV // N_HEAD
    diagonal = lax.broadcasted_iota(jnp.int32, (BDEV, BDEV), 0) == lax.broadcasted_iota(jnp.int32, (BDEV, BDEV), 1)

    def visit_block(text_dirs, shard_index):
        image_block = lax.dynamic_index_in_dim(image_units, shard_index, 0, keepdims=False)
        quarter_sums = jnp.zeros((N_HEAD, BDEV, P_SIZE), jnp.float32)
        for offset in range(STEPS):
            owner_shard = ((shard_index + offset) % N_DP).astype(jnp.int32)
            text_block = lax.dynamic_index_in_dim(text_units, owner_shard, 0, keepdims=False)
            logits = logit_scale * jnp.dot(image_block, text_block.T, preferred_element_type=jnp.float32) + logit_bias
            if offset == 0:
                labels = jnp.where(diagonal, jnp.float32(1.0), jnp.float32(-1.0))
            else:
                labels = -jnp.ones((BDEV, BDEV), jnp.float32)
            pair_weights = (-labels * jax.nn.sigmoid(-labels * logits)).astype(jnp.bfloat16)
            quarter_sums = quarter_sums + jnp.einsum('iqj,qjp->qip', pair_weights.reshape(BDEV, N_HEAD, quarter_rows).astype(jnp.float32), text_block.reshape(N_HEAD, quarter_rows, P_SIZE).astype(jnp.float32))
            text_term = logit_scale * jnp.dot(pair_weights.T, image_block, preferred_element_type=jnp.float32)
            current = lax.dynamic_index_in_dim(text_dirs, owner_shard, 0, keepdims=False)
            text_dirs = lax.dynamic_update_index_in_dim(text_dirs, current + text_term, owner_shard, 0)
        rounded = lax.optimization_barrier((logit_scale * quarter_sums).astype(jnp.bfloat16))
        return (text_dirs, lax.optimization_barrier(jnp.sum(rounded.astype(jnp.float32), axis=0)))
    text_dirs, image_dirs = lax.scan(visit_block, jnp.zeros((N_DP, BDEV, P_SIZE), jnp.float32), jnp.arange(N_DP, dtype=jnp.int32))
    image_tangent = tangent(image_dirs.reshape(BATCH, P_SIZE), image_unit_f, image_inverse).astype(jnp.bfloat16)
    text_tangent = tangent(text_dirs.reshape(BATCH, P_SIZE), text_unit_f, text_inverse).astype(jnp.bfloat16)
    image_proj_grad = jnp.dot(image_features.T, image_tangent, preferred_element_type=jnp.float32)
    text_proj_grad = jnp.dot(text_features.T, text_tangent, preferred_element_type=jnp.float32)
    return (image_proj_grad, text_proj_grad)
```

```python
import jax
import jax.numpy as jnp
from jax import lax
from jax.sharding import Mesh, PartitionSpec as P

STEPS = 8
X, YL, YH, C = 4, 4, 2, 2
DP = ("z", "x", "yl")

epsilon = 1e-06
bf16 = jnp.bfloat16
f32 = jnp.float32


def from_ahead(block, distance):
    count = lax.axis_size(DP)
    return lax.ppermute(block, DP, [((i + distance) % count, i) for i in range(count)])


def swapped(block, axis):
    return lax.ppermute(block, axis, [(0, 1), (1, 0)])


def spread(block, axis):
    count = lax.axis_size(axis)
    return lax.all_to_all(
        jnp.broadcast_to(block[None], (count,) + block.shape), axis, 0, 0, tiled=True
    )


def window(quarter, sign):
    held = quarter
    for distance in (1, 2, 4):
        held = jnp.concatenate([held, from_ahead(held, sign * distance)], axis=0)
    return held


def half_pair(array, c):
    half = array.shape[-2] // 2
    mine = lax.dynamic_slice_in_dim(array, c * half, half, array.ndim - 2)
    other = lax.dynamic_slice_in_dim(array, (1 - c) * half, half, array.ndim - 2)
    return mine, other


def directions(rows, others, first_row, scale, bias):
    logits = scale * jnp.einsum("ip,jp->ij", rows, others, preferred_element_type=f32) + bias
    quarter = others.shape[0] // STEPS
    row_index = lax.broadcasted_iota(jnp.int32, logits.shape, 0)
    col_index = lax.broadcasted_iota(jnp.int32, logits.shape, 1)
    matched = (col_index < quarter) & (row_index == col_index + first_row)
    labels = jnp.where(matched, f32(1.0), f32(-1.0))
    weights = (-labels * jax.nn.sigmoid(-labels * logits)).astype(bf16)
    return scale * jnp.dot(weights, others, preferred_element_type=f32)


def per_device(image_features, text_features, image_proj, text_proj, log_scale, logit_bias):
    yh, c = lax.axis_index("yh"), lax.axis_index("c")
    rows_all, slice_width = image_features.shape
    width = image_proj.shape[1]
    half, quarter = rows_all // 2, rows_all // 4
    scale = jnp.exp(log_scale)

    def projected(mine):
        picked = [half_pair(features, c)[0 if mine else 1] for features in (image_features, text_features)]
        return [
            jnp.dot(rows, weight, preferred_element_type=f32)
            for rows, weight in zip(picked, (image_proj, text_proj))
        ]

    away = jnp.stack([value.astype(bf16) for value in projected(False)])
    came = swapped(away, "c").astype(f32)
    pair_sum = (jnp.stack(projected(True)) + came).astype(bf16)
    split = pair_sum.reshape(2, 2, quarter, width)
    needed_there = lax.dynamic_index_in_dim(split, 1 - yh, 1, keepdims=False)
    needed_here = lax.dynamic_index_in_dim(split, yh, 1, keepdims=False)
    got_own = swapped(needed_there, "yh")

    def normalize(raw):
        inverse = lax.rsqrt(jnp.sum(raw * raw, axis=-1, keepdims=True) + epsilon)
        return raw * inverse, inverse

    own_raw = needed_here.astype(f32) + got_own.astype(f32)
    own_unit, own_inverse = normalize(own_raw)
    own_block = own_unit.astype(bf16)
    got_other = swapped(needed_here, "yh")
    other_raw = needed_there.astype(f32) + got_other.astype(f32)
    other_unit, other_inverse = normalize(other_raw)

    text_window = window(own_block[1], 1)
    image_window = window(own_block[0], -1)

    def in_order(own, other):
        first = jnp.where(yh == 0, own, other)
        second = jnp.where(yh == 0, other, own)
        return jnp.concatenate([first, second], axis=1)

    unit = in_order(own_unit, other_unit)
    inverse = in_order(own_inverse, other_inverse)
    block_all = lax.all_gather(unit.astype(bf16), "c", axis=1, tiled=True)

    first_row = c * half + yh * quarter
    image_part = directions(block_all[0], text_window, first_row, scale, logit_bias)
    text_part = directions(block_all[1], image_window, first_row, scale, logit_bias)
    parts = jnp.stack([image_part, text_part])
    mine, other = half_pair(parts, c)
    chip_sum = mine + swapped(other.astype(bf16), "c").astype(f32)
    direction = chip_sum + swapped(chip_sum.astype(bf16), "yh").astype(f32)
    tangent = (
        (direction - unit * jnp.sum(unit * direction, axis=-1, keepdims=True)) * inverse
    ).astype(bf16)
    tangent_all = lax.all_gather(tangent, "c", axis=1, tiled=True)

    grads = jnp.concatenate(
        [
            jnp.einsum("rd,rp->dp", features, tangent_all[tower], preferred_element_type=f32)
            for tower, features in enumerate((image_features, text_features))
        ],
        axis=0,
    ).astype(bf16)

    nz = lax.axis_size("z")
    got = lax.all_to_all(grads.reshape(X, -1, width), "x", 0, 0, tiled=True)
    part = jnp.sum(got.astype(f32), axis=0).astype(bf16)
    got = lax.all_to_all(part.reshape(nz, -1, width), "z", 0, 0, tiled=True)
    part = jnp.sum(got.astype(f32), axis=0).astype(bf16)
    part = jnp.sum(spread(part, "yl").astype(f32), axis=0).astype(bf16)
    part = spread(part, "z").reshape(-1, width)
    total = spread(part, "x").reshape(2, slice_width, width).astype(f32)
    return total[0], total[1]


def solution(mesh):
    dp = mesh.shape["dp"]
    fine = Mesh(
        mesh.devices.reshape(dp // (X * YL), X, YL, YH, C), ("z", "x", "yl", "yh", "c")
    )
    head = ("yh", "c")
    placed = (P(DP, head), P(DP, head), P(head, None), P(head, None), P(), P())
    return jax.shard_map(
        per_device,
        mesh=fine,
        in_specs=placed,
        out_specs=(P(head, None), P(head, None)),
        check_vma=False,
    )
```

```python
import jax
import jax.numpy as jnp
from jax import lax
from jax.sharding import Mesh, PartitionSpec as P

STEPS = 8
X, YL, YH, C = 4, 4, 2, 2
DP = ("z", "x", "yl")

epsilon = 1e-06
bf16 = jnp.bfloat16
f32 = jnp.float32


def from_ahead(block, distance):
    count = lax.axis_size(DP)
    return lax.ppermute(block, DP, [((i + distance) % count, i) for i in range(count)])


def swapped(block, axis):
    return lax.ppermute(block, axis, [(0, 1), (1, 0)])


def spread(block, axis):
    count = lax.axis_size(axis)
    return lax.all_to_all(
        jnp.broadcast_to(block[None], (count,) + block.shape), axis, 0, 0, tiled=True
    )


def half_pair(array, c):
    half = array.shape[-2] // 2
    mine = lax.dynamic_slice_in_dim(array, c * half, half, array.ndim - 2)
    other = lax.dynamic_slice_in_dim(array, (1 - c) * half, half, array.ndim - 2)
    return mine, other


def directions(rows, others, first_row, scale, bias):
    logits = scale * jnp.einsum("ip,jp->ij", rows, others, preferred_element_type=f32) + bias
    quarter = others.shape[0] // STEPS
    row_index = lax.broadcasted_iota(jnp.int32, logits.shape, 0)
    col_index = lax.broadcasted_iota(jnp.int32, logits.shape, 1)
    matched = (col_index < quarter) & (row_index == col_index + first_row)
    labels = jnp.where(matched, f32(1.0), f32(-1.0))
    weights = (-labels * jax.nn.sigmoid(-labels * logits)).astype(bf16)
    return scale * jnp.dot(weights, others, preferred_element_type=f32)


def per_device(image_features, text_features, image_proj, text_proj, log_scale, logit_bias):
    yh, c = lax.axis_index("yh"), lax.axis_index("c")
    rows_all, slice_width = image_features.shape
    width = image_proj.shape[1]
    half, quarter = rows_all // 2, rows_all // 4
    scale = jnp.exp(log_scale)

    features = {"text": text_features, "image": image_features}
    weights = {"text": text_proj, "image": image_proj}
    towers = ("text", "image")

    needed_there, needed_here = {}, {}
    for t in towers:
        mine, other = half_pair(features[t], c)
        away = jnp.dot(other, weights[t], preferred_element_type=f32).astype(bf16)
        came = swapped(away, "c").astype(f32)
        pair_sum = (jnp.dot(mine, weights[t], preferred_element_type=f32) + came).astype(bf16)
        needed_there[t] = lax.dynamic_slice_in_dim(pair_sum, (1 - yh) * quarter, quarter, 0)
        needed_here[t] = lax.dynamic_slice_in_dim(pair_sum, yh * quarter, quarter, 0)

    def normalize(raw):
        inverse = lax.rsqrt(jnp.sum(raw * raw, axis=-1, keepdims=True) + epsilon)
        return raw * inverse, inverse

    own_unit, own_inverse, held = {}, {}, {}
    for t in towers:
        own_raw = needed_here[t].astype(f32) + swapped(needed_there[t], "yh").astype(f32)
        own_unit[t], own_inverse[t] = normalize(own_raw)
        held[t] = own_unit[t].astype(bf16)

    sign = {"text": 1, "image": -1}
    for t in towers:
        block = held[t]
        block = jnp.concatenate([block, from_ahead(block, sign[t] * 2)], axis=0)
        block = jnp.concatenate([block, from_ahead(block, sign[t])], axis=0)
        late, block = lax.optimization_barrier((needed_here[t], block))
        needed_here[t] = late
        held[t] = jnp.concatenate([block, from_ahead(block, sign[t] * 4)], axis=0)

    def in_order(own, other):
        first = jnp.where(yh == 0, own, other)
        second = jnp.where(yh == 0, other, own)
        return jnp.concatenate([first, second], axis=0)

    unit, inverse, rows = {}, {}, {}
    for t in towers:
        other_raw = needed_there[t].astype(f32) + swapped(needed_here[t], "yh").astype(f32)
        other_unit, other_inverse = normalize(other_raw)
        unit[t] = in_order(own_unit[t], other_unit)
        inverse[t] = in_order(own_inverse[t], other_inverse)
        rows[t] = lax.all_gather(unit[t].astype(bf16), "c", axis=0, tiled=True)

    first_row = c * half + yh * quarter
    opposite = {"text": "image", "image": "text"}
    scattered = {}
    for t in ("image", "text"):
        part = directions(rows[t], held[opposite[t]], first_row, scale, logit_bias)
        mine, other = half_pair(part, c)
        chip_sum = mine + swapped(other.astype(bf16), "c").astype(f32)
        direction = chip_sum + swapped(chip_sum.astype(bf16), "yh").astype(f32)
        tangent = (
            (direction - unit[t] * jnp.sum(unit[t] * direction, axis=-1, keepdims=True))
            * inverse[t]
        ).astype(bf16)
        tangent_all = lax.all_gather(tangent, "c", axis=0, tiled=True)
        grad = jnp.einsum("rd,rp->dp", features[t], tangent_all, preferred_element_type=f32)
        got = lax.all_to_all(grad.astype(bf16).reshape(X, -1, width), "x", 0, 0, tiled=True)
        scattered[t] = jnp.sum(got.astype(f32), axis=0).astype(bf16)

    nz = lax.axis_size("z")
    part = jnp.concatenate([scattered["image"], scattered["text"]], axis=0)
    got = lax.all_to_all(part.reshape(nz, -1, width), "z", 0, 0, tiled=True)
    part = jnp.sum(got.astype(f32), axis=0).astype(bf16)
    part = jnp.sum(spread(part, "yl").astype(f32), axis=0).astype(bf16)
    part = spread(part, "z").reshape(-1, width)
    total = spread(part, "x").reshape(X, 2, -1, width).astype(f32)
    return tuple(total[:, tower].reshape(slice_width, width) for tower in range(2))


def solution(mesh):
    dp = mesh.shape["dp"]
    fine = Mesh(
        mesh.devices.reshape(dp // (X * YL), X, YL, YH, C), ("z", "x", "yl", "yh", "c")
    )
    head = ("yh", "c")
    placed = (P(DP, head), P(DP, head), P(head, None), P(head, None), P(), P())
    return jax.shard_map(
        per_device,
        mesh=fine,
        in_specs=placed,
        out_specs=(P(head, None), P(head, None)),
        check_vma=False,
    )
```

```python
import jax
import jax.numpy as jnp
from jax import lax
from jax.sharding import Mesh, PartitionSpec as P

STEPS = 8
X, YL, YH, C = 4, 4, 2, 2
LANES = 128
DP = ("z", "x", "yl")

epsilon = 1e-06
bf16 = jnp.bfloat16
f32 = jnp.float32


def from_ahead(block, distance):
    count = lax.axis_size(DP)
    return lax.ppermute(block, DP, [((i + distance) % count, i) for i in range(count)])


def swapped(block, axis):
    return lax.ppermute(block, axis, [(0, 1), (1, 0)])


def spread(block, axis):
    count = lax.axis_size(axis)
    return lax.all_to_all(
        jnp.broadcast_to(block[None], (count,) + block.shape), axis, 0, 0, tiled=True
    )


def half_pair(array, c):
    half = array.shape[-2] // 2
    mine = lax.dynamic_slice_in_dim(array, c * half, half, array.ndim - 2)
    other = lax.dynamic_slice_in_dim(array, (1 - c) * half, half, array.ndim - 2)
    return mine, other


def directions(rows, blocks, first_row, scale, bias):
    total = None
    for number, block in enumerate(blocks):
        logits = scale * jnp.einsum("ip,jp->ij", rows, block, preferred_element_type=f32) + bias
        labels = f32(-1.0)
        if number == 0:
            quarter = rows.shape[0] // 4
            row_index = lax.broadcasted_iota(jnp.int32, logits.shape, 0)
            col_index = lax.broadcasted_iota(jnp.int32, logits.shape, 1)
            matched = (col_index < quarter) & (row_index == col_index + first_row)
            labels = jnp.where(matched, f32(1.0), f32(-1.0))
        weights = (-labels * jax.nn.sigmoid(-labels * logits)).astype(bf16)
        part = jnp.dot(weights, block, preferred_element_type=f32)
        total = part if total is None else total + part
    return scale * total


def lanes_first(rows):
    return rows.reshape(rows.shape[0], -1, LANES).swapaxes(0, 1)


def scattered_over_x(grad):
    got = lax.all_to_all(
        grad.astype(bf16).reshape(X, -1, grad.shape[1]), "x", 0, 0, tiled=True
    )
    return jnp.sum(got.astype(f32), axis=0).astype(bf16)


def summed_over_the_rest(part):
    part = lanes_first(part)
    tiles, height, _ = part.shape
    nz = lax.axis_size("z")
    piece = -(-tiles * height // (8 * nz)) * 8
    flat = jnp.pad(part.reshape(-1, LANES), ((0, nz * piece - tiles * height), (0, 0)))
    got = lax.all_to_all(flat.reshape(nz, piece, LANES), "z", 0, 0, tiled=True)
    part = jnp.sum(got.astype(f32), axis=0).astype(bf16)
    part = jnp.sum(spread(part, "yl").astype(f32), axis=0).astype(bf16)
    part = spread(part, "z").reshape(-1, LANES)[: tiles * height].reshape(tiles, height, LANES)
    total = spread(part, "x").reshape(X, tiles, 2, height // 2, LANES)
    total = total.transpose(2, 0, 3, 1, 4).astype(f32)
    return [total[tower].reshape(X * height // 2, tiles * LANES) for tower in range(2)]


def per_device(image_features, text_features, image_proj, text_proj, log_scale, logit_bias):
    yh, c = lax.axis_index("yh"), lax.axis_index("c")
    rows_all, slice_width = image_features.shape
    width = image_proj.shape[1]
    half, quarter = rows_all // 2, rows_all // 4
    scale = jnp.exp(log_scale)

    features = {"text": text_features, "image": image_features}
    weights = {"text": text_proj, "image": image_proj}
    towers = ("text", "image")

    halves = {t: half_pair(features[t], c) for t in towers}
    away = jnp.stack(
        [jnp.dot(halves[t][1], weights[t], preferred_element_type=f32).astype(bf16) for t in towers]
    )
    came = swapped(away, "c").astype(f32)
    needed_there, needed_here = {}, {}
    for number, t in enumerate(towers):
        own_sum = jnp.dot(halves[t][0], weights[t], preferred_element_type=f32)
        pair_sum = (own_sum + came[number]).astype(bf16)
        needed_there[t] = lax.dynamic_slice_in_dim(pair_sum, (1 - yh) * quarter, quarter, 0)
        needed_here[t] = lax.dynamic_slice_in_dim(pair_sum, yh * quarter, quarter, 0)

    def normalize(raw):
        inverse = lax.rsqrt(jnp.sum(raw * raw, axis=-1, keepdims=True) + epsilon)
        return raw * inverse, inverse

    own_unit, own_inverse, held = {}, {}, {}
    for t in towers:
        own_raw = needed_here[t].astype(f32) + swapped(needed_there[t], "yh").astype(f32)
        own_unit[t], own_inverse[t] = normalize(own_raw)
        held[t] = own_unit[t].astype(bf16)

    sign = {"text": 1, "image": -1}
    for t in towers:
        block = held[t]
        block = jnp.concatenate([block, from_ahead(block, sign[t] * 2)], axis=0)
        held[t] = jnp.concatenate([block, from_ahead(block, sign[t])], axis=0)
    to_complete = jnp.stack([needed_here[t] for t in towers])
    to_complete, held = lax.optimization_barrier((to_complete, held))
    completing = swapped(to_complete, "yh").astype(f32)
    held = {t: (held[t], from_ahead(held[t], sign[t] * 4)) for t in towers}

    def in_order(own, other):
        first = jnp.where(yh == 0, own, other)
        second = jnp.where(yh == 0, other, own)
        return jnp.concatenate([first, second], axis=0)

    unit, inverse, rows = {}, {}, {}
    for number, t in enumerate(towers):
        other_raw = needed_there[t].astype(f32) + completing[number]
        other_unit, other_inverse = normalize(other_raw)
        unit[t] = in_order(own_unit[t], other_unit)
        inverse[t] = in_order(own_inverse[t], other_inverse)
        rows[t] = lax.all_gather(unit[t].astype(bf16), "c", axis=0, tiled=True)

    first_row = c * half + yh * quarter
    opposite = {"text": "image", "image": "text"}
    earlier = None
    grads = {}
    for t in ("image", "text"):
        part = directions(rows[t], held[opposite[t]], first_row, scale, logit_bias)
        mine, other = half_pair(part, c)
        chip_sum = mine + swapped(other.astype(bf16), "c").astype(f32)
        away = chip_sum.astype(bf16)
        if earlier is not None:
            away, earlier = lax.optimization_barrier((away, earlier))
        earlier = swapped(away, "yh")
        direction = chip_sum + earlier.astype(f32)
        tangent = (
            (direction - unit[t] * jnp.sum(unit[t] * direction, axis=-1, keepdims=True))
            * inverse[t]
        ).astype(bf16)
        tangent_all = lax.all_gather(tangent, "c", axis=0, tiled=True)
        grads[t] = jnp.einsum("rd,rp->dp", features[t], tangent_all, preferred_element_type=f32)
    parts = [scattered_over_x(grads[t]) for t in ("image", "text")]
    image_total, text_total = summed_over_the_rest(jnp.concatenate(parts, axis=0))
    return image_total, text_total


def solution(mesh):
    dp = mesh.shape["dp"]
    fine = Mesh(
        mesh.devices.reshape(dp // (X * YL), X, YL, YH, C), ("z", "x", "yl", "yh", "c")
    )
    head = ("yh", "c")
    placed = (P(DP, head), P(DP, head), P(head, None), P(head, None), P(), P())
    return jax.shard_map(
        per_device,
        mesh=fine,
        in_specs=placed,
        out_specs=(P(head, None), P(head, None)),
        check_vma=False,
    )
```

```python
import jax
import jax.numpy as jnp
from jax import lax
from jax.experimental import pallas as pl
from jax.experimental.pallas import tpu as pltpu
from jax.sharding import Mesh, PartitionSpec as P

STEPS = 8
X, YL, YH, C = 4, 4, 2, 2
LANES = 128
DP = ("z", "x", "yl")

epsilon = 1e-06
bf16 = jnp.bfloat16
f32 = jnp.float32


def from_ahead(block, distance):
    count = lax.axis_size(DP)
    return lax.ppermute(block, DP, [((i + distance) % count, i) for i in range(count)])


def swapped(block, axis):
    return lax.ppermute(block, axis, [(0, 1), (1, 0)])


def spread(block, axis):
    count = lax.axis_size(axis)
    return lax.all_to_all(
        jnp.broadcast_to(block[None], (count,) + block.shape), axis, 0, 0, tiled=True
    )


def half_pair(array, c):
    half = array.shape[-2] // 2
    mine = lax.dynamic_slice_in_dim(array, c * half, half, array.ndim - 2)
    other = lax.dynamic_slice_in_dim(array, (1 - c) * half, half, array.ndim - 2)
    return mine, other


VMEM = pl.BlockSpec(memory_space=pltpu.VMEM)
SMEM = pl.BlockSpec(memory_space=pltpu.SMEM)
VMEM_LIMIT = 32 * 2**20


def directions_kernel(place, numbers, rows_ref, first_ref, second_ref, mine_ref, other_ref):
    c, yh = place[0], place[1]
    scale, bias = numbers[0], numbers[1]
    half = mine_ref.shape[0]
    quarter = half // 2
    for kept in (False, True):
        start = pl.multiple_of((c if kept else 1 - c) * half, half)
        rows = rows_ref[pl.ds(start, half), :]
        total = None
        for block_ref in (first_ref, second_ref):
            block = block_ref[...]
            logits = (
                scale
                * lax.dot_general(
                    rows, block, (((1,), (1,)), ((), ())), preferred_element_type=f32
                )
                + bias
            )
            if kept and block_ref is first_ref:
                row = lax.broadcasted_iota(jnp.int32, logits.shape, 0)
                col = lax.broadcasted_iota(jnp.int32, logits.shape, 1)
                matched = (col < quarter) & (row == col + yh * quarter)
                value = jax.nn.sigmoid(jnp.where(matched, -logits, logits))
                pair_weights = jnp.where(matched, -value, value)
            else:
                pair_weights = jax.nn.sigmoid(logits)
            part = jnp.dot(pair_weights.astype(bf16), block, preferred_element_type=f32)
            total = part if total is None else total + part
        if kept:
            mine_ref[...] = scale * total
        else:
            other_ref[...] = (scale * total).astype(bf16)


def directions(place, numbers, rows, blocks):
    count, width = rows.shape
    half = count // 2
    pairs = count * sum(block.shape[0] for block in blocks)
    return pl.pallas_call(
        directions_kernel,
        out_shape=(
            jax.ShapeDtypeStruct((half, width), f32),
            jax.ShapeDtypeStruct((half, width), bf16),
        ),
        in_specs=[SMEM, SMEM, VMEM, VMEM, VMEM],
        out_specs=(VMEM, VMEM),
        compiler_params=pltpu.CompilerParams(vmem_limit_bytes=VMEM_LIMIT),
        cost_estimate=pl.CostEstimate(
            flops=4 * pairs * width, bytes_accessed=10 * count * width, transcendentals=pairs
        ),
    )(place, numbers, rows, *blocks)


def tangent_kernel(mine_ref, came_ref, got_ref, unit_ref, inverse_ref, out_ref):
    unit = unit_ref[...]
    direction = mine_ref[...] + came_ref[...].astype(f32) + got_ref[...].astype(f32)
    along = jnp.sum(unit * direction, axis=-1, keepdims=True)
    out_ref[...] = ((direction - unit * along) * inverse_ref[...]).astype(bf16)


def tangent(mine, came, got, unit, inverse):
    return pl.pallas_call(
        tangent_kernel,
        out_shape=jax.ShapeDtypeStruct(mine.shape, bf16),
        in_specs=[VMEM] * 5,
        out_specs=VMEM,
        compiler_params=pltpu.CompilerParams(vmem_limit_bytes=VMEM_LIMIT),
        cost_estimate=pl.CostEstimate(
            flops=8 * mine.size, bytes_accessed=14 * mine.size, transcendentals=0
        ),
    )(mine, came, got, unit, inverse)


def lanes_first(rows):
    return rows.reshape(rows.shape[0], -1, LANES).swapaxes(0, 1)


def scattered_over_x(grad):
    got = lax.all_to_all(
        grad.astype(bf16).reshape(X, -1, grad.shape[1]), "x", 0, 0, tiled=True
    )
    return jnp.sum(got.astype(f32), axis=0).astype(bf16)


def summed_over_the_rest(part):
    part = lanes_first(part)
    tiles, height, _ = part.shape
    nz = lax.axis_size("z")
    piece = -(-tiles * height // (8 * nz)) * 8
    flat = jnp.pad(part.reshape(-1, LANES), ((0, nz * piece - tiles * height), (0, 0)))
    got = lax.all_to_all(flat.reshape(nz, piece, LANES), "z", 0, 0, tiled=True)
    part = jnp.sum(got.astype(f32), axis=0).astype(bf16)
    part = jnp.sum(spread(part, "yl").astype(f32), axis=0).astype(bf16)
    part = spread(part, "z").reshape(-1, LANES)[: tiles * height].reshape(tiles, height, LANES)
    part = part.swapaxes(0, 1).reshape(height, tiles * LANES)
    total = spread(part, "x").reshape(X, 2, height // 2, -1).astype(f32)
    return [total[:, tower].reshape(X * height // 2, -1) for tower in range(2)]


def per_device(image_features, text_features, image_proj, text_proj, log_scale, logit_bias):
    yh, c = lax.axis_index("yh"), lax.axis_index("c")
    rows_all, slice_width = image_features.shape
    width = image_proj.shape[1]
    half, quarter = rows_all // 2, rows_all // 4
    scale = jnp.exp(log_scale)

    features = {"text": text_features, "image": image_features}
    weights = {"text": text_proj, "image": image_proj}
    towers = ("text", "image")

    halves = {t: half_pair(features[t], c) for t in towers}
    away = jnp.stack(
        [jnp.dot(halves[t][1], weights[t], preferred_element_type=f32).astype(bf16) for t in towers]
    )
    came = swapped(away, "c").astype(f32)
    needed_there, needed_here = {}, {}
    for number, t in enumerate(towers):
        own_sum = jnp.dot(halves[t][0], weights[t], preferred_element_type=f32)
        pair_sum = (own_sum + came[number]).astype(bf16)
        needed_there[t] = lax.dynamic_slice_in_dim(pair_sum, (1 - yh) * quarter, quarter, 0)
        needed_here[t] = lax.dynamic_slice_in_dim(pair_sum, yh * quarter, quarter, 0)

    def normalize(raw):
        inverse = lax.rsqrt(jnp.sum(raw * raw, axis=-1, keepdims=True) + epsilon)
        return raw * inverse, inverse

    got_own = swapped(jnp.stack([needed_there[t] for t in towers]), "yh").astype(f32)
    own_unit, own_inverse, held = {}, {}, {}
    for number, t in enumerate(towers):
        own_raw = needed_here[t].astype(f32) + got_own[number]
        own_unit[t], own_inverse[t] = normalize(own_raw)
        held[t] = own_unit[t].astype(bf16)

    sign = {"text": 1, "image": -1}
    for distance in (2, 1):
        held = {
            t: jnp.concatenate([held[t], from_ahead(held[t], sign[t] * distance)], axis=0)
            for t in towers
        }
        if distance == 2:
            held = lax.optimization_barrier(held)
    to_complete = jnp.stack([needed_here[t] for t in towers])
    to_complete, held["text"] = lax.optimization_barrier((to_complete, held["text"]))
    completing = swapped(to_complete, "yh").astype(f32)
    held = lax.optimization_barrier(held)
    held = {t: (held[t], from_ahead(held[t], sign[t] * 4)) for t in towers}

    def in_order(own, other):
        first = jnp.where(yh == 0, own, other)
        second = jnp.where(yh == 0, other, own)
        return jnp.concatenate([first, second], axis=0)

    unit, inverse, rows = {}, {}, {}
    for number, t in enumerate(towers):
        other_raw = needed_there[t].astype(f32) + completing[number]
        other_unit, other_inverse = normalize(other_raw)
        unit[t] = in_order(own_unit[t], other_unit)
        inverse[t] = in_order(own_inverse[t], other_inverse)
        rows[t] = lax.all_gather(unit[t].astype(bf16), "c", axis=0, tiled=True)

    place = jnp.stack([c, yh]).astype(jnp.int32)
    numbers = jnp.stack([scale, logit_bias])
    opposite = {"text": "image", "image": "text"}
    earlier = None
    grads = {}
    for t in ("image", "text"):
        mine, other = directions(place, numbers, rows[t], held[opposite[t]])
        came = swapped(other, "c")
        away = (mine + came.astype(f32)).astype(bf16)
        if earlier is not None:
            away, earlier = lax.optimization_barrier((away, earlier))
        earlier = swapped(away, "yh")
        tangents = tangent(mine, came, earlier, unit[t], inverse[t])
        tangent_all = lax.all_gather(tangents, "c", axis=0, tiled=True)
        grads[t] = jnp.einsum("rd,rp->dp", features[t], tangent_all, preferred_element_type=f32)
    parts = [scattered_over_x(grads[t]) for t in ("image", "text")]
    image_total, text_total = summed_over_the_rest(jnp.concatenate(parts, axis=0))
    return image_total, text_total


def solution(mesh):
    dp = mesh.shape["dp"]
    fine = Mesh(
        mesh.devices.reshape(dp // (X * YL), X, YL, YH, C), ("z", "x", "yl", "yh", "c")
    )
    head = ("yh", "c")
    placed = (P(DP, head), P(DP, head), P(head, None), P(head, None), P(), P())
    return jax.shard_map(
        per_device,
        mesh=fine,
        in_specs=placed,
        out_specs=(P(head, None), P(head, None)),
        check_vma=False,
    )
```

```python
import jax
import jax.numpy as jnp
from jax import lax
from jax.experimental import pallas as pl
from jax.experimental.pallas import tpu as pltpu
from jax.sharding import Mesh, PartitionSpec as P

STEPS = 8
X, YL, YH, C = 4, 4, 2, 2
LANES = 128
DP = ("z", "x", "yl")

epsilon = 1e-06
bf16 = jnp.bfloat16
f32 = jnp.float32


def from_ahead(block, distance):
    count = lax.axis_size(DP)
    return lax.ppermute(block, DP, [((i + distance) % count, i) for i in range(count)])


def swapped(block, axis):
    return lax.ppermute(block, axis, [(0, 1), (1, 0)])


def spread(block, axis):
    count = lax.axis_size(axis)
    return lax.all_to_all(
        jnp.broadcast_to(block[None], (count,) + block.shape), axis, 0, 0, tiled=True
    )


def half_pair(array, c):
    half = array.shape[-2] // 2
    mine = lax.dynamic_slice_in_dim(array, c * half, half, array.ndim - 2)
    other = lax.dynamic_slice_in_dim(array, (1 - c) * half, half, array.ndim - 2)
    return mine, other


VMEM = pl.BlockSpec(memory_space=pltpu.VMEM)
SMEM = pl.BlockSpec(memory_space=pltpu.SMEM)
VMEM_LIMIT = 32 * 2**20


def directions_kernel(place, numbers, rows_ref, first_ref, second_ref, mine_ref, other_ref):
    c, yh = place[0], place[1]
    scale, bias = numbers[0], numbers[1]
    half = mine_ref.shape[0]
    quarter = half // 2
    for kept in (False, True):
        start = pl.multiple_of((c if kept else 1 - c) * half, half)
        rows = rows_ref[pl.ds(start, half), :]
        total = None
        for block_ref in (first_ref, second_ref):
            block = block_ref[...]
            logits = (
                scale
                * lax.dot_general(
                    rows, block, (((1,), (1,)), ((), ())), preferred_element_type=f32
                )
                + bias
            )
            if kept and block_ref is first_ref:
                row = lax.broadcasted_iota(jnp.int32, logits.shape, 0)
                col = lax.broadcasted_iota(jnp.int32, logits.shape, 1)
                matched = (col < quarter) & (row == col + yh * quarter)
                value = jax.nn.sigmoid(jnp.where(matched, -logits, logits))
                pair_weights = jnp.where(matched, -value, value)
            else:
                pair_weights = jax.nn.sigmoid(logits)
            part = jnp.dot(pair_weights.astype(bf16), block, preferred_element_type=f32)
            total = part if total is None else total + part
        if kept:
            mine_ref[...] = scale * total
        else:
            other_ref[...] = (scale * total).astype(bf16)


def directions(place, numbers, rows, blocks):
    count, width = rows.shape
    half = count // 2
    pairs = count * sum(block.shape[0] for block in blocks)
    return pl.pallas_call(
        directions_kernel,
        out_shape=(
            jax.ShapeDtypeStruct((half, width), f32),
            jax.ShapeDtypeStruct((half, width), bf16),
        ),
        in_specs=[SMEM, SMEM, VMEM, VMEM, VMEM],
        out_specs=(VMEM, VMEM),
        compiler_params=pltpu.CompilerParams(vmem_limit_bytes=VMEM_LIMIT),
        cost_estimate=pl.CostEstimate(
            flops=4 * pairs * width, bytes_accessed=10 * count * width, transcendentals=pairs
        ),
    )(place, numbers, rows, *blocks)


def tangent_kernel(mine_ref, came_ref, got_ref, unit_ref, inverse_ref, out_ref):
    unit = unit_ref[...]
    direction = mine_ref[...] + came_ref[...].astype(f32) + got_ref[...].astype(f32)
    along = jnp.sum(unit * direction, axis=-1, keepdims=True)
    out_ref[...] = ((direction - unit * along) * inverse_ref[...]).astype(bf16)


def tangent(mine, came, got, unit, inverse):
    return pl.pallas_call(
        tangent_kernel,
        out_shape=jax.ShapeDtypeStruct(mine.shape, bf16),
        in_specs=[VMEM] * 5,
        out_specs=VMEM,
        compiler_params=pltpu.CompilerParams(vmem_limit_bytes=VMEM_LIMIT),
        cost_estimate=pl.CostEstimate(
            flops=8 * mine.size, bytes_accessed=14 * mine.size, transcendentals=0
        ),
    )(mine, came, got, unit, inverse)


def lanes_first(rows):
    return rows.reshape(rows.shape[0], -1, LANES).swapaxes(0, 1)


def scattered_over_x(grad):
    got = lax.all_to_all(
        grad.astype(bf16).reshape(X, -1, grad.shape[1]), "x", 0, 0, tiled=True
    )
    return jnp.sum(got.astype(f32), axis=0).astype(bf16)


def summed_over_the_rest(part):
    part = lanes_first(part)
    tiles, height, _ = part.shape
    across = ("z", "yl")
    count = lax.axis_size(across)
    piece = -(-tiles * height // (8 * count)) * 8
    flat = jnp.pad(part.reshape(-1, LANES), ((0, count * piece - tiles * height), (0, 0)))
    got = lax.all_to_all(flat.reshape(count, piece, LANES), across, 0, 0, tiled=True)
    part = jnp.sum(got.astype(f32), axis=0).astype(bf16)
    part = spread(part, across).reshape(-1, LANES)[: tiles * height]
    part = part.reshape(tiles, height, LANES).swapaxes(0, 1).reshape(height, tiles * LANES)
    total = spread(part, "x").reshape(X, 2, height // 2, -1).astype(f32)
    return [total[:, tower].reshape(X * height // 2, -1) for tower in range(2)]


def per_device(image_features, text_features, image_proj, text_proj, log_scale, logit_bias):
    yh, c = lax.axis_index("yh"), lax.axis_index("c")
    rows_all, slice_width = image_features.shape
    width = image_proj.shape[1]
    half, quarter = rows_all // 2, rows_all // 4
    scale = jnp.exp(log_scale)

    features = {"text": text_features, "image": image_features}
    weights = {"text": text_proj, "image": image_proj}
    towers = ("text", "image")

    halves = {t: half_pair(features[t], c) for t in towers}
    away = jnp.stack(
        [jnp.dot(halves[t][1], weights[t], preferred_element_type=f32).astype(bf16) for t in towers]
    )
    came = swapped(away, "c").astype(f32)
    needed_there, needed_here = {}, {}
    for number, t in enumerate(towers):
        own_sum = jnp.dot(halves[t][0], weights[t], preferred_element_type=f32)
        pair_sum = (own_sum + came[number]).astype(bf16)
        needed_there[t] = lax.dynamic_slice_in_dim(pair_sum, (1 - yh) * quarter, quarter, 0)
        needed_here[t] = lax.dynamic_slice_in_dim(pair_sum, yh * quarter, quarter, 0)

    def normalize(raw):
        inverse = lax.rsqrt(jnp.sum(raw * raw, axis=-1, keepdims=True) + epsilon)
        return raw * inverse, inverse

    own_unit, own_inverse, held = {}, {}, {}
    for t in towers:
        own_raw = needed_here[t].astype(f32) + swapped(needed_there[t], "yh").astype(f32)
        own_unit[t], own_inverse[t] = normalize(own_raw)
        held[t] = own_unit[t].astype(bf16)

    sign = {"text": 1, "image": -1}
    for t in towers:
        for distance in (2, 1):
            held[t] = jnp.concatenate([held[t], from_ahead(held[t], sign[t] * distance)], axis=0)
    to_complete, _ = lax.optimization_barrier(
        (jnp.stack([needed_here[t] for t in towers]), held)
    )
    completing = swapped(to_complete, "yh").astype(f32)
    held = {t: (held[t], from_ahead(held[t], sign[t] * 4)) for t in towers}

    def in_order(own, other):
        first = jnp.where(yh == 0, own, other)
        second = jnp.where(yh == 0, other, own)
        return jnp.concatenate([first, second], axis=0)

    unit, inverse, rows = {}, {}, {}
    for number, t in enumerate(towers):
        other_raw = needed_there[t].astype(f32) + completing[number]
        other_unit, other_inverse = normalize(other_raw)
        unit[t] = in_order(own_unit[t], other_unit)
        inverse[t] = in_order(own_inverse[t], other_inverse)
        rows[t] = lax.all_gather(unit[t].astype(bf16), "c", axis=0, tiled=True)

    place = jnp.stack([c, yh]).astype(jnp.int32)
    numbers = jnp.stack([scale, logit_bias])
    opposite = {"text": "image", "image": "text"}
    earlier = None
    grads = {}
    for t in ("image", "text"):
        mine, other = directions(place, numbers, rows[t], held[opposite[t]])
        came = swapped(other, "c")
        away = (mine + came.astype(f32)).astype(bf16)
        if earlier is not None:
            away, earlier = lax.optimization_barrier((away, earlier))
        earlier = swapped(away, "yh")
        tangents = tangent(mine, came, earlier, unit[t], inverse[t])
        tangent_all = lax.all_gather(tangents, "c", axis=0, tiled=True)
        grads[t] = jnp.einsum("rd,rp->dp", features[t], tangent_all, preferred_element_type=f32)
    parts = [scattered_over_x(grads[t]) for t in ("image", "text")]
    image_total, text_total = summed_over_the_rest(jnp.concatenate(parts, axis=0))
    return image_total, text_total


def solution(mesh):
    dp = mesh.shape["dp"]
    fine = Mesh(
        mesh.devices.reshape(dp // (X * YL), X, YL, YH, C), ("z", "x", "yl", "yh", "c")
    )
    head = ("yh", "c")
    placed = (P(DP, head), P(DP, head), P(head, None), P(head, None), P(), P())
    return jax.shard_map(
        per_device,
        mesh=fine,
        in_specs=placed,
        out_specs=(P(head, None), P(head, None)),
        check_vma=False,
    )
```

```python
import jax
import jax.numpy as jnp
from jax import lax
from jax.experimental import pallas as pl
from jax.experimental.pallas import tpu as pltpu
from jax.sharding import Mesh, PartitionSpec as P

STEPS = 8
X, YL, YH, C = 4, 4, 2, 2
LANES = 128
DP = ("z", "x", "yl")

epsilon = 1e-06
bf16 = jnp.bfloat16
f32 = jnp.float32


def from_ahead(block, distance):
    count = lax.axis_size(DP)
    return lax.ppermute(block, DP, [((i + distance) % count, i) for i in range(count)])


def swapped(block, axis):
    return lax.ppermute(block, axis, [(0, 1), (1, 0)])


def spread(block, axis):
    count = lax.axis_size(axis)
    return lax.all_to_all(
        jnp.broadcast_to(block[None], (count,) + block.shape), axis, 0, 0, tiled=True
    )


def half_pair(array, c):
    half = array.shape[-2] // 2
    mine = lax.dynamic_slice_in_dim(array, c * half, half, array.ndim - 2)
    other = lax.dynamic_slice_in_dim(array, (1 - c) * half, half, array.ndim - 2)
    return mine, other


VMEM = pl.BlockSpec(memory_space=pltpu.VMEM)
SMEM = pl.BlockSpec(memory_space=pltpu.SMEM)
VMEM_LIMIT = 32 * 2**20


def directions_kernel(place, numbers, rows_ref, first_ref, second_ref, mine_ref, other_ref):
    c, yh = place[0], place[1]
    scale, bias = numbers[0], numbers[1]
    half = mine_ref.shape[0]
    quarter = half // 2
    for kept in (False, True):
        start = pl.multiple_of((c if kept else 1 - c) * half, half)
        rows = rows_ref[pl.ds(start, half), :]
        total = None
        for block_ref in (first_ref, second_ref):
            block = block_ref[...]
            logits = (
                scale
                * lax.dot_general(
                    rows, block, (((1,), (1,)), ((), ())), preferred_element_type=f32
                )
                + bias
            )
            if kept and block_ref is first_ref:
                row = lax.broadcasted_iota(jnp.int32, logits.shape, 0)
                col = lax.broadcasted_iota(jnp.int32, logits.shape, 1)
                matched = (col < quarter) & (row == col + yh * quarter)
                value = jax.nn.sigmoid(jnp.where(matched, -logits, logits))
                pair_weights = jnp.where(matched, -value, value)
            else:
                pair_weights = jax.nn.sigmoid(logits)
            part = jnp.dot(pair_weights.astype(bf16), block, preferred_element_type=f32)
            total = part if total is None else total + part
        if kept:
            mine_ref[...] = scale * total
        else:
            other_ref[...] = (scale * total).astype(bf16)


def directions(place, numbers, rows, blocks):
    count, width = rows.shape
    half = count // 2
    pairs = count * sum(block.shape[0] for block in blocks)
    return pl.pallas_call(
        directions_kernel,
        out_shape=(
            jax.ShapeDtypeStruct((half, width), f32),
            jax.ShapeDtypeStruct((half, width), bf16),
        ),
        in_specs=[SMEM, SMEM, VMEM, VMEM, VMEM],
        out_specs=(VMEM, VMEM),
        compiler_params=pltpu.CompilerParams(vmem_limit_bytes=VMEM_LIMIT),
        cost_estimate=pl.CostEstimate(
            flops=4 * pairs * width, bytes_accessed=10 * count * width, transcendentals=pairs
        ),
    )(place, numbers, rows, *blocks)


def tangent_kernel(mine_ref, came_ref, got_ref, unit_ref, inverse_ref, out_ref):
    unit = unit_ref[...]
    direction = mine_ref[...] + came_ref[...].astype(f32) + got_ref[...].astype(f32)
    along = jnp.sum(unit * direction, axis=-1, keepdims=True)
    out_ref[...] = ((direction - unit * along) * inverse_ref[...]).astype(bf16)


def tangent(mine, came, got, unit, inverse):
    return pl.pallas_call(
        tangent_kernel,
        out_shape=jax.ShapeDtypeStruct(mine.shape, bf16),
        in_specs=[VMEM] * 5,
        out_specs=VMEM,
        compiler_params=pltpu.CompilerParams(vmem_limit_bytes=VMEM_LIMIT),
        cost_estimate=pl.CostEstimate(
            flops=8 * mine.size, bytes_accessed=14 * mine.size, transcendentals=0
        ),
    )(mine, came, got, unit, inverse)


def lanes_first(rows):
    return rows.reshape(rows.shape[0], -1, LANES).swapaxes(0, 1)


def scattered_over_x(grad):
    got = lax.all_to_all(
        grad.astype(bf16).reshape(X, -1, grad.shape[1]), "x", 0, 0, tiled=True
    )
    return jnp.sum(got.astype(f32), axis=0).astype(bf16)


def summed_over_the_rest(part):
    part = lanes_first(part)
    tiles, height, _ = part.shape
    across = ("z", "yl")
    count = lax.axis_size(across)
    piece = -(-tiles * height // (8 * count)) * 8
    flat = jnp.pad(part.reshape(-1, LANES), ((0, count * piece - tiles * height), (0, 0)))
    got = lax.all_to_all(flat.reshape(count, piece, LANES), across, 0, 0, tiled=True)
    part = jnp.sum(got.astype(f32), axis=0).astype(bf16)
    part = spread(part, across).reshape(-1, LANES)[: tiles * height]
    part = part.reshape(tiles, height, LANES).swapaxes(0, 1).reshape(height, tiles * LANES)
    total = spread(part, "x").reshape(X, 2, height // 2, -1).astype(f32)
    return [total[:, tower].reshape(X * height // 2, -1) for tower in range(2)]


def per_device(image_features, text_features, image_proj, text_proj, log_scale, logit_bias):
    yh, c = lax.axis_index("yh"), lax.axis_index("c")
    rows_all, slice_width = image_features.shape
    width = image_proj.shape[1]
    half, quarter = rows_all // 2, rows_all // 4
    scale = jnp.exp(log_scale)

    features = {"text": text_features, "image": image_features}
    weights = {"text": text_proj, "image": image_proj}
    towers = ("text", "image")

    halves = {t: half_pair(features[t], c) for t in towers}
    away = jnp.stack(
        [jnp.dot(halves[t][1], weights[t], preferred_element_type=f32).astype(bf16) for t in towers]
    )
    came = swapped(away, "c").astype(f32)
    needed_there, needed_here = {}, {}
    for number, t in enumerate(towers):
        own_sum = jnp.dot(halves[t][0], weights[t], preferred_element_type=f32)
        pair_sum = (own_sum + came[number]).astype(bf16)
        needed_there[t] = lax.dynamic_slice_in_dim(pair_sum, (1 - yh) * quarter, quarter, 0)
        needed_here[t] = lax.dynamic_slice_in_dim(pair_sum, yh * quarter, quarter, 0)

    def normalize(raw):
        inverse = lax.rsqrt(jnp.sum(raw * raw, axis=-1, keepdims=True) + epsilon)
        return raw * inverse, inverse

    own_unit, own_inverse, held = {}, {}, {}
    for t in towers:
        own_raw = needed_here[t].astype(f32) + swapped(needed_there[t], "yh").astype(f32)
        own_unit[t], own_inverse[t] = normalize(own_raw)
        held[t] = own_unit[t].astype(bf16)

    held_own = dict(held)

    sign = {"text": 1, "image": -1}
    for t in towers:
        for distance in (2, 1):
            held[t] = jnp.concatenate([held[t], from_ahead(held[t], sign[t] * distance)], axis=0)
    completing = {}
    for t in ("image", "text"):
        to_complete, _ = lax.optimization_barrier((needed_here[t], held))
        completing[t] = swapped(to_complete, "yh").astype(f32)
    held = {t: (held[t], from_ahead(held[t], sign[t] * 4)) for t in towers}

    def in_order(own, other):
        first = jnp.where(yh == 0, own, other)
        second = jnp.where(yh == 0, other, own)
        return jnp.concatenate([first, second], axis=0)

    place = jnp.stack([c, yh]).astype(jnp.int32)
    numbers = jnp.stack([scale, logit_bias])
    opposite = {"text": "image", "image": "text"}
    grads = {}
    came, earlier = None, None
    for t in ("image", "text"):
        other_raw = needed_there[t].astype(f32) + completing[t]
        if came is not None:
            other_raw, _ = lax.optimization_barrier((other_raw, came))
        other_unit, other_inverse = normalize(other_raw)
        rows = lax.all_gather(
            in_order(held_own[t], other_unit.astype(bf16)), "c", axis=0, tiled=True
        )
        mine, other = directions(place, numbers, rows, held[opposite[t]])
        came = swapped(other, "c")
        away = (mine + came.astype(f32)).astype(bf16)
        if earlier is not None:
            away, earlier = lax.optimization_barrier((away, earlier))
        later_unit, later_inverse, _ = lax.optimization_barrier((other_unit, other_inverse, came))
        unit = in_order(own_unit[t], later_unit)
        inverse = in_order(own_inverse[t], later_inverse)
        earlier = swapped(away, "yh")
        tangents = tangent(mine, came, earlier, unit, inverse)
        tangent_all = lax.all_gather(tangents, "c", axis=0, tiled=True)
        grads[t] = jnp.einsum("rd,rp->dp", features[t], tangent_all, preferred_element_type=f32)
    parts = [scattered_over_x(grads[t]) for t in ("image", "text")]
    image_total, text_total = summed_over_the_rest(jnp.concatenate(parts, axis=0))
    return image_total, text_total


def solution(mesh):
    dp = mesh.shape["dp"]
    fine = Mesh(
        mesh.devices.reshape(dp // (X * YL), X, YL, YH, C), ("z", "x", "yl", "yh", "c")
    )
    head = ("yh", "c")
    placed = (P(DP, head), P(DP, head), P(head, None), P(head, None), P(), P())
    return jax.shard_map(
        per_device,
        mesh=fine,
        in_specs=placed,
        out_specs=(P(head, None), P(head, None)),
        check_vma=False,
    )
```

```python
import jax
import jax.numpy as jnp
from jax import lax
from jax.experimental import pallas as pl
from jax.experimental.pallas import tpu as pltpu
from jax.sharding import Mesh, PartitionSpec as P

STEPS = 8
X, YL, YH, C = 4, 4, 2, 2
LANES = 128
DP = ("z", "x", "yl")

epsilon = 1e-06
bf16 = jnp.bfloat16
f32 = jnp.float32


def from_ahead(block, distance):
    count = lax.axis_size(DP)
    return lax.ppermute(block, DP, [((i + distance) % count, i) for i in range(count)])


def swapped(block, axis):
    return lax.ppermute(block, axis, [(0, 1), (1, 0)])


def spread(block, axis):
    count = lax.axis_size(axis)
    return lax.all_to_all(
        jnp.broadcast_to(block[None], (count,) + block.shape), axis, 0, 0, tiled=True
    )


def half_pair(array, c):
    half = array.shape[-2] // 2
    mine = lax.dynamic_slice_in_dim(array, c * half, half, array.ndim - 2)
    other = lax.dynamic_slice_in_dim(array, (1 - c) * half, half, array.ndim - 2)
    return mine, other


VMEM = pl.BlockSpec(memory_space=pltpu.VMEM)
SMEM = pl.BlockSpec(memory_space=pltpu.SMEM)
VMEM_LIMIT = 32 * 2**20


def directions_kernel(place, numbers, rows_ref, first_ref, second_ref, mine_ref, other_ref):
    c, yh = place[0], place[1]
    scale, bias = numbers[0], numbers[1]
    half = mine_ref.shape[0]
    quarter = half // 2
    for kept in (False, True):
        start = pl.multiple_of((c if kept else 1 - c) * half, half)
        rows = rows_ref[pl.ds(start, half), :]
        total = None
        for block_ref in (first_ref, second_ref):
            block = block_ref[...]
            logits = (
                scale
                * lax.dot_general(
                    rows, block, (((1,), (1,)), ((), ())), preferred_element_type=f32
                )
                + bias
            )
            if kept and block_ref is first_ref:
                row = lax.broadcasted_iota(jnp.int32, logits.shape, 0)
                col = lax.broadcasted_iota(jnp.int32, logits.shape, 1)
                matched = (col < quarter) & (row == col + yh * quarter)
                value = jax.nn.sigmoid(jnp.where(matched, -logits, logits))
                pair_weights = jnp.where(matched, -value, value)
            else:
                pair_weights = jax.nn.sigmoid(logits)
            part = jnp.dot(pair_weights.astype(bf16), block, preferred_element_type=f32)
            total = part if total is None else total + part
        if kept:
            mine_ref[...] = scale * total
        else:
            other_ref[...] = (scale * total).astype(bf16)


def directions(place, numbers, rows, blocks):
    count, width = rows.shape
    half = count // 2
    pairs = count * sum(block.shape[0] for block in blocks)
    return pl.pallas_call(
        directions_kernel,
        out_shape=(
            jax.ShapeDtypeStruct((half, width), f32),
            jax.ShapeDtypeStruct((half, width), bf16),
        ),
        in_specs=[SMEM, SMEM, VMEM, VMEM, VMEM],
        out_specs=(VMEM, VMEM),
        compiler_params=pltpu.CompilerParams(vmem_limit_bytes=VMEM_LIMIT),
        cost_estimate=pl.CostEstimate(
            flops=4 * pairs * width, bytes_accessed=10 * count * width, transcendentals=pairs
        ),
    )(place, numbers, rows, *blocks)


def tangent_kernel(mine_ref, came_ref, got_ref, unit_ref, inverse_ref, out_ref):
    unit = unit_ref[...]
    direction = mine_ref[...] + came_ref[...].astype(f32) + got_ref[...].astype(f32)
    along = jnp.sum(unit * direction, axis=-1, keepdims=True)
    out_ref[...] = ((direction - unit * along) * inverse_ref[...]).astype(bf16)


def tangent(mine, came, got, unit, inverse):
    return pl.pallas_call(
        tangent_kernel,
        out_shape=jax.ShapeDtypeStruct(mine.shape, bf16),
        in_specs=[VMEM] * 5,
        out_specs=VMEM,
        compiler_params=pltpu.CompilerParams(vmem_limit_bytes=VMEM_LIMIT),
        cost_estimate=pl.CostEstimate(
            flops=8 * mine.size, bytes_accessed=14 * mine.size, transcendentals=0
        ),
    )(mine, came, got, unit, inverse)


def lanes_first(rows):
    return rows.reshape(rows.shape[0], -1, LANES).swapaxes(0, 1)


def scattered_over_x(grad):
    got = lax.all_to_all(
        grad.astype(bf16).reshape(X, -1, grad.shape[1]), "x", 0, 0, tiled=True
    )
    return jnp.sum(got.astype(f32), axis=0).astype(bf16)


def summed_over_the_rest(part):
    part = lanes_first(part)
    tiles, height, _ = part.shape
    across = ("z", "yl")
    count = lax.axis_size(across)
    piece = -(-tiles * height // (8 * count)) * 8
    flat = jnp.pad(part.reshape(-1, LANES), ((0, count * piece - tiles * height), (0, 0)))
    got = lax.all_to_all(flat.reshape(count, piece, LANES), across, 0, 0, tiled=True)
    part = jnp.sum(got.astype(f32), axis=0).astype(bf16)
    part = spread(part, across).reshape(-1, LANES)[: tiles * height]
    part = part.reshape(tiles, height, LANES).swapaxes(0, 1).reshape(height, tiles * LANES)
    total = spread(part, "x").reshape(X, 2, height // 2, -1).astype(f32)
    return [total[:, tower].reshape(X * height // 2, -1) for tower in range(2)]


def per_device(image_features, text_features, image_proj, text_proj, log_scale, logit_bias):
    yh, c = lax.axis_index("yh"), lax.axis_index("c")
    rows_all, slice_width = image_features.shape
    width = image_proj.shape[1]
    half, quarter = rows_all // 2, rows_all // 4
    scale = jnp.exp(log_scale)

    features = {"text": text_features, "image": image_features}
    weights = {"text": text_proj, "image": image_proj}
    towers = ("text", "image")

    halves = {t: half_pair(features[t], c) for t in towers}
    away = jnp.stack(
        [jnp.dot(halves[t][1], weights[t], preferred_element_type=f32).astype(bf16) for t in towers]
    )
    came = swapped(away, "c").astype(f32)
    needed_there, needed_here = {}, {}
    for number, t in enumerate(towers):
        own_sum = jnp.dot(halves[t][0], weights[t], preferred_element_type=f32)
        pair_sum = (own_sum + came[number]).astype(bf16)
        needed_there[t] = lax.dynamic_slice_in_dim(pair_sum, (1 - yh) * quarter, quarter, 0)
        needed_here[t] = lax.dynamic_slice_in_dim(pair_sum, yh * quarter, quarter, 0)

    def normalize(raw):
        inverse = lax.rsqrt(jnp.sum(raw * raw, axis=-1, keepdims=True) + epsilon)
        return raw * inverse, inverse

    own_unit, own_inverse, held = {}, {}, {}
    for t in towers:
        own_raw = needed_here[t].astype(f32) + swapped(needed_there[t], "yh").astype(f32)
        own_unit[t], own_inverse[t] = normalize(own_raw)
        held[t] = own_unit[t].astype(bf16)

    sign = {"text": 1, "image": -1}
    for t in towers:
        near = [from_ahead(held[t], sign[t] * distance) for distance in (2, 3, 1)]
        held[t] = jnp.concatenate([held[t], *near], axis=0)
    to_complete, _ = lax.optimization_barrier(
        (jnp.stack([needed_here[t] for t in towers]), held)
    )
    completing = swapped(to_complete, "yh").astype(f32)
    held = {t: (held[t], from_ahead(held[t], sign[t] * 4)) for t in towers}

    def in_order(own, other):
        first = jnp.where(yh == 0, own, other)
        second = jnp.where(yh == 0, other, own)
        return jnp.concatenate([first, second], axis=0)

    unit, inverse, rows = {}, {}, {}
    for number, t in enumerate(towers):
        other_raw = needed_there[t].astype(f32) + completing[number]
        other_unit, other_inverse = normalize(other_raw)
        unit[t] = in_order(own_unit[t], other_unit)
        inverse[t] = in_order(own_inverse[t], other_inverse)
        rows[t] = lax.all_gather(unit[t].astype(bf16), "c", axis=0, tiled=True)

    place = jnp.stack([c, yh]).astype(jnp.int32)
    numbers = jnp.stack([scale, logit_bias])
    opposite = {"text": "image", "image": "text"}
    sums, away, got, grads = {}, {}, {}, {}
    for t in ("image", "text"):
        mine, other = directions(place, numbers, rows[t], held[opposite[t]])
        sums[t] = mine, swapped(other, "c")
        away[t] = (mine + sums[t][1].astype(f32)).astype(bf16)
    got["image"] = swapped(away["image"], "yh")
    got["image"], away["text"] = lax.optimization_barrier((got["image"], away["text"]))
    got["text"] = swapped(away["text"], "yh")
    for t in ("image", "text"):
        tangents = tangent(*sums[t], got[t], unit[t], inverse[t])
        tangent_all = lax.all_gather(tangents, "c", axis=0, tiled=True)
        grads[t] = jnp.einsum("rd,rp->dp", features[t], tangent_all, preferred_element_type=f32)
    parts = [scattered_over_x(grads[t]) for t in ("image", "text")]
    image_total, text_total = summed_over_the_rest(jnp.concatenate(parts, axis=0))
    return image_total, text_total


def solution(mesh):
    dp = mesh.shape["dp"]
    fine = Mesh(
        mesh.devices.reshape(dp // (X * YL), X, YL, YH, C), ("z", "x", "yl", "yh", "c")
    )
    head = ("yh", "c")
    placed = (P(DP, head), P(DP, head), P(head, None), P(head, None), P(), P())
    return jax.shard_map(
        per_device,
        mesh=fine,
        in_specs=placed,
        out_specs=(P(head, None), P(head, None)),
        check_vma=False,
    )
```

```python
import jax
import jax.numpy as jnp
from jax import lax
from jax.experimental import pallas as pl
from jax.experimental.pallas import tpu as pltpu
from jax.sharding import Mesh, PartitionSpec as P

STEPS = 8
X, YL, YH, C = 4, 4, 2, 2
LANES = 128
DP = ("z", "x", "yl")

epsilon = 1e-06
bf16 = jnp.bfloat16
f32 = jnp.float32


def from_ahead(block, distance):
    count = lax.axis_size(DP)
    return lax.ppermute(block, DP, [((i + distance) % count, i) for i in range(count)])


def swapped(block, axis):
    return lax.ppermute(block, axis, [(0, 1), (1, 0)])


def spread(block, axis):
    count = lax.axis_size(axis)
    return lax.all_to_all(
        jnp.broadcast_to(block[None], (count,) + block.shape), axis, 0, 0, tiled=True
    )


def half_pair(array, c):
    half = array.shape[-2] // 2
    mine = lax.dynamic_slice_in_dim(array, c * half, half, array.ndim - 2)
    other = lax.dynamic_slice_in_dim(array, (1 - c) * half, half, array.ndim - 2)
    return mine, other


VMEM = pl.BlockSpec(memory_space=pltpu.VMEM)
SMEM = pl.BlockSpec(memory_space=pltpu.SMEM)
VMEM_LIMIT = 32 * 2**20


def other_halves_kernel(core, *refs):
    *refs, out_ref = refs
    towers = out_ref.shape[0]
    half = out_ref.shape[1]
    start = pl.multiple_of((1 - core[0]) * half, half)
    for number in range(towers):
        features_ref, weights_ref = refs[number], refs[towers + number]
        out_ref[number] = jnp.dot(
            features_ref[pl.ds(start, half), :], weights_ref[...], preferred_element_type=f32
        ).astype(bf16)


def other_halves(c, features, weights):
    count, depth = features[0].shape
    width = weights[0].shape[1]
    towers = len(features)
    return pl.pallas_call(
        other_halves_kernel,
        out_shape=jax.ShapeDtypeStruct((towers, count // 2, width), bf16),
        in_specs=[SMEM] + [VMEM] * (2 * towers),
        out_specs=VMEM,
        compiler_params=pltpu.CompilerParams(vmem_limit_bytes=VMEM_LIMIT),
        cost_estimate=pl.CostEstimate(
            flops=towers * count * depth * width,
            bytes_accessed=2 * towers * (depth * width + count * depth + count * width // 2),
            transcendentals=0,
        ),
    )(jnp.reshape(c, (1,)).astype(jnp.int32), *features, *weights)


def directions_kernel(place, numbers, rows_ref, first_ref, second_ref, mine_ref, other_ref):
    c, yh = place[0], place[1]
    scale, bias = numbers[0], numbers[1]
    half = mine_ref.shape[0]
    quarter = half // 2
    for kept in (False, True):
        start = pl.multiple_of((c if kept else 1 - c) * half, half)
        rows = rows_ref[pl.ds(start, half), :]
        total = None
        for block_ref in (first_ref, second_ref):
            block = block_ref[...]
            logits = (
                scale
                * lax.dot_general(
                    rows, block, (((1,), (1,)), ((), ())), preferred_element_type=f32
                )
                + bias
            )
            if kept and block_ref is first_ref:
                row = lax.broadcasted_iota(jnp.int32, logits.shape, 0)
                col = lax.broadcasted_iota(jnp.int32, logits.shape, 1)
                matched = (col < quarter) & (row == col + yh * quarter)
                value = jax.nn.sigmoid(jnp.where(matched, -logits, logits))
                pair_weights = jnp.where(matched, -value, value)
            else:
                pair_weights = jax.nn.sigmoid(logits)
            part = jnp.dot(pair_weights.astype(bf16), block, preferred_element_type=f32)
            total = part if total is None else total + part
        if kept:
            mine_ref[...] = scale * total
        else:
            other_ref[...] = (scale * total).astype(bf16)


def directions(place, numbers, rows, blocks):
    count, width = rows.shape
    half = count // 2
    pairs = count * sum(block.shape[0] for block in blocks)
    return pl.pallas_call(
        directions_kernel,
        out_shape=(
            jax.ShapeDtypeStruct((half, width), f32),
            jax.ShapeDtypeStruct((half, width), bf16),
        ),
        in_specs=[SMEM, SMEM, VMEM, VMEM, VMEM],
        out_specs=(VMEM, VMEM),
        compiler_params=pltpu.CompilerParams(vmem_limit_bytes=VMEM_LIMIT),
        cost_estimate=pl.CostEstimate(
            flops=4 * pairs * width, bytes_accessed=10 * count * width, transcendentals=pairs
        ),
    )(place, numbers, rows, *blocks)


def tangent_kernel(mine_ref, came_ref, got_ref, unit_ref, inverse_ref, out_ref):
    unit = unit_ref[...]
    direction = mine_ref[...] + came_ref[...].astype(f32) + got_ref[...].astype(f32)
    along = jnp.sum(unit * direction, axis=-1, keepdims=True)
    out_ref[...] = ((direction - unit * along) * inverse_ref[...]).astype(bf16)


def tangent(mine, came, got, unit, inverse):
    return pl.pallas_call(
        tangent_kernel,
        out_shape=jax.ShapeDtypeStruct(mine.shape, bf16),
        in_specs=[VMEM] * 5,
        out_specs=VMEM,
        compiler_params=pltpu.CompilerParams(vmem_limit_bytes=VMEM_LIMIT),
        cost_estimate=pl.CostEstimate(
            flops=8 * mine.size, bytes_accessed=14 * mine.size, transcendentals=0
        ),
    )(mine, came, got, unit, inverse)


def lanes_first(rows):
    return rows.reshape(rows.shape[0], -1, LANES).swapaxes(0, 1)


def scattered_over_x(grad):
    got = lax.all_to_all(
        grad.astype(bf16).reshape(X, -1, grad.shape[1]), "x", 0, 0, tiled=True
    )
    return jnp.sum(got.astype(f32), axis=0).astype(bf16)


def summed_over_the_rest(part):
    part = lanes_first(part)
    tiles, height, _ = part.shape
    across = ("z", "yl")
    count = lax.axis_size(across)
    piece = -(-tiles * height // (8 * count)) * 8
    flat = jnp.pad(part.reshape(-1, LANES), ((0, count * piece - tiles * height), (0, 0)))
    got = lax.all_to_all(flat.reshape(count, piece, LANES), across, 0, 0, tiled=True)
    part = jnp.sum(got.astype(f32), axis=0).astype(bf16)
    part = spread(part, across).reshape(-1, LANES)[: tiles * height]
    part = part.reshape(tiles, height, LANES).swapaxes(0, 1).reshape(height, tiles * LANES)
    total = spread(part, "x").reshape(X, 2, height // 2, -1).astype(f32)
    return [total[:, tower].reshape(X * height // 2, -1) for tower in range(2)]


def per_device(image_features, text_features, image_proj, text_proj, log_scale, logit_bias):
    yh, c = lax.axis_index("yh"), lax.axis_index("c")
    rows_all, slice_width = image_features.shape
    width = image_proj.shape[1]
    half, quarter = rows_all // 2, rows_all // 4
    scale = jnp.exp(log_scale)

    features = {"text": text_features, "image": image_features}
    weights = {"text": text_proj, "image": image_proj}
    towers = ("text", "image")

    halves = {t: half_pair(features[t], c) for t in towers}
    away = other_halves(c, [features[t] for t in towers], [weights[t] for t in towers])
    came = swapped(away, "c").astype(f32)
    needed_there, needed_here = {}, {}
    for number, t in enumerate(towers):
        own_sum = jnp.dot(halves[t][0], weights[t], preferred_element_type=f32)
        pair_sum = (own_sum + came[number]).astype(bf16)
        needed_there[t] = lax.dynamic_slice_in_dim(pair_sum, (1 - yh) * quarter, quarter, 0)
        needed_here[t] = lax.dynamic_slice_in_dim(pair_sum, yh * quarter, quarter, 0)

    def normalize(raw):
        inverse = lax.rsqrt(jnp.sum(raw * raw, axis=-1, keepdims=True) + epsilon)
        return raw * inverse, inverse

    own_unit, own_inverse, held = {}, {}, {}
    for t in towers:
        own_raw = needed_here[t].astype(f32) + swapped(needed_there[t], "yh").astype(f32)
        own_unit[t], own_inverse[t] = normalize(own_raw)
        held[t] = own_unit[t].astype(bf16)

    sign = {"text": 1, "image": -1}
    near = {
        t: [from_ahead(held[t], sign[t] * distance) for distance in (2, 3, 1)] for t in towers
    }
    to_complete, _ = lax.optimization_barrier(
        (jnp.stack([needed_here[t] for t in towers]), [near[t][0] for t in towers])
    )
    held = {t: jnp.concatenate([held[t], *near[t]], axis=0) for t in towers}
    completing = swapped(to_complete, "yh").astype(f32)
    held = {t: (held[t], from_ahead(held[t], sign[t] * 4)) for t in towers}

    def in_order(own, other):
        first = jnp.where(yh == 0, own, other)
        second = jnp.where(yh == 0, other, own)
        return jnp.concatenate([first, second], axis=0)

    unit, inverse, rows = {}, {}, {}
    for number, t in enumerate(towers):
        other_raw = needed_there[t].astype(f32) + completing[number]
        other_unit, other_inverse = normalize(other_raw)
        unit[t] = in_order(own_unit[t], other_unit)
        inverse[t] = in_order(own_inverse[t], other_inverse)
        rows[t] = lax.all_gather(unit[t].astype(bf16), "c", axis=0, tiled=True)

    place = jnp.stack([c, yh]).astype(jnp.int32)
    numbers = jnp.stack([scale, logit_bias])
    opposite = {"text": "image", "image": "text"}
    sums, away, got, grads = {}, {}, {}, {}
    for t in ("image", "text"):
        if t == "text":
            rows[t], _ = lax.optimization_barrier((rows[t], sums["image"][1]))
        mine, other = directions(place, numbers, rows[t], held[opposite[t]])
        sums[t] = mine, swapped(other, "c")
        away[t] = (mine + sums[t][1].astype(f32)).astype(bf16)
    got["image"] = swapped(away["image"], "yh")
    got["image"], away["text"] = lax.optimization_barrier((got["image"], away["text"]))
    got["text"] = swapped(away["text"], "yh")
    for t in ("image", "text"):
        tangents = tangent(*sums[t], got[t], unit[t], inverse[t])
        tangent_all = lax.all_gather(tangents, "c", axis=0, tiled=True)
        grads[t] = jnp.einsum("rd,rp->dp", features[t], tangent_all, preferred_element_type=f32)
    parts = [scattered_over_x(grads[t]) for t in ("image", "text")]
    image_total, text_total = summed_over_the_rest(jnp.concatenate(parts, axis=0))
    return image_total, text_total


def solution(mesh):
    dp = mesh.shape["dp"]
    fine = Mesh(
        mesh.devices.reshape(dp // (X * YL), X, YL, YH, C), ("z", "x", "yl", "yh", "c")
    )
    head = ("yh", "c")
    placed = (P(DP, head), P(DP, head), P(head, None), P(head, None), P(), P())
    return jax.shard_map(
        per_device,
        mesh=fine,
        in_specs=placed,
        out_specs=(P(head, None), P(head, None)),
        check_vma=False,
    )
```

```python
import jax
import jax.numpy as jnp
from jax import lax
from jax.experimental import pallas as pl
from jax.experimental.pallas import tpu as pltpu
from jax.sharding import Mesh, PartitionSpec as P

STEPS = 8
X, YL, YH, C = 4, 4, 2, 2
LANES = 128
DP = ("z", "x", "yl")

epsilon = 1e-06
bf16 = jnp.bfloat16
f32 = jnp.float32


def from_ahead(block, distance):
    count = lax.axis_size(DP)
    return lax.ppermute(block, DP, [((i + distance) % count, i) for i in range(count)])


def swapped(block, axis):
    return lax.ppermute(block, axis, [(0, 1), (1, 0)])


def spread(block, axis):
    count = lax.axis_size(axis)
    return lax.all_to_all(
        jnp.broadcast_to(block[None], (count,) + block.shape), axis, 0, 0, tiled=True
    )


def half_pair(array, c):
    half = array.shape[-2] // 2
    mine = lax.dynamic_slice_in_dim(array, c * half, half, array.ndim - 2)
    other = lax.dynamic_slice_in_dim(array, (1 - c) * half, half, array.ndim - 2)
    return mine, other


VMEM = pl.BlockSpec(memory_space=pltpu.VMEM)
SMEM = pl.BlockSpec(memory_space=pltpu.SMEM)
VMEM_LIMIT = 32 * 2**20


def directions_kernel(place, numbers, rows_ref, first_ref, second_ref, mine_ref, other_ref):
    c, yh = place[0], place[1]
    scale, bias = numbers[0], numbers[1]
    half = mine_ref.shape[0]
    quarter = half // 2
    for kept in (False, True):
        start = pl.multiple_of((c if kept else 1 - c) * half, half)
        rows = rows_ref[pl.ds(start, half), :]
        total = None
        for block_ref in (first_ref, second_ref):
            block = block_ref[...]
            logits = (
                scale
                * lax.dot_general(
                    rows, block, (((1,), (1,)), ((), ())), preferred_element_type=f32
                )
                + bias
            )
            if kept and block_ref is first_ref:
                row = lax.broadcasted_iota(jnp.int32, logits.shape, 0)
                col = lax.broadcasted_iota(jnp.int32, logits.shape, 1)
                matched = (col < quarter) & (row == col + yh * quarter)
                value = jax.nn.sigmoid(jnp.where(matched, -logits, logits))
                pair_weights = jnp.where(matched, -value, value)
            else:
                pair_weights = jax.nn.sigmoid(logits)
            part = jnp.dot(pair_weights.astype(bf16), block, preferred_element_type=f32)
            total = part if total is None else total + part
        if kept:
            mine_ref[...] = scale * total
        else:
            other_ref[...] = (scale * total).astype(bf16)


def directions(place, numbers, rows, blocks):
    count, width = rows.shape
    half = count // 2
    pairs = count * sum(block.shape[0] for block in blocks)
    return pl.pallas_call(
        directions_kernel,
        out_shape=(
            jax.ShapeDtypeStruct((half, width), f32),
            jax.ShapeDtypeStruct((half, width), bf16),
        ),
        in_specs=[SMEM, SMEM, VMEM, VMEM, VMEM],
        out_specs=(VMEM, VMEM),
        compiler_params=pltpu.CompilerParams(vmem_limit_bytes=VMEM_LIMIT),
        cost_estimate=pl.CostEstimate(
            flops=4 * pairs * width, bytes_accessed=10 * count * width, transcendentals=pairs
        ),
    )(place, numbers, rows, *blocks)


def tangent_kernel(mine_ref, came_ref, got_ref, unit_ref, inverse_ref, out_ref):
    unit = unit_ref[...]
    direction = mine_ref[...] + came_ref[...].astype(f32) + got_ref[...].astype(f32)
    along = jnp.sum(unit * direction, axis=-1, keepdims=True)
    out_ref[...] = ((direction - unit * along) * inverse_ref[...]).astype(bf16)


def tangent(mine, came, got, unit, inverse):
    return pl.pallas_call(
        tangent_kernel,
        out_shape=jax.ShapeDtypeStruct(mine.shape, bf16),
        in_specs=[VMEM] * 5,
        out_specs=VMEM,
        compiler_params=pltpu.CompilerParams(vmem_limit_bytes=VMEM_LIMIT),
        cost_estimate=pl.CostEstimate(
            flops=8 * mine.size, bytes_accessed=14 * mine.size, transcendentals=0
        ),
    )(mine, came, got, unit, inverse)


def lanes_first(rows):
    return rows.reshape(rows.shape[0], -1, LANES).swapaxes(0, 1)


def scattered_over_x(grad):
    got = lax.all_to_all(
        grad.astype(bf16).reshape(X, -1, grad.shape[1]), "x", 0, 0, tiled=True
    )
    return jnp.sum(got.astype(f32), axis=0).astype(bf16)


def summed_over_the_rest(part):
    part = lanes_first(part)
    tiles, height, _ = part.shape
    across = ("z", "yl")
    count = lax.axis_size(across)
    piece = -(-tiles * height // (8 * count)) * 8
    flat = jnp.pad(part.reshape(-1, LANES), ((0, count * piece - tiles * height), (0, 0)))
    got = lax.all_to_all(flat.reshape(count, piece, LANES), across, 0, 0, tiled=True)
    part = jnp.sum(got.astype(f32), axis=0).astype(bf16)
    part = spread(part, across).reshape(-1, LANES)[: tiles * height]
    part = part.reshape(tiles, height, LANES).swapaxes(0, 1).reshape(height, tiles * LANES)
    total = spread(part, "x").reshape(X, 2, height // 2, -1).astype(f32)
    return [total[:, tower].reshape(X * height // 2, -1) for tower in range(2)]


def per_device(image_features, text_features, image_proj, text_proj, log_scale, logit_bias):
    yh, c = lax.axis_index("yh"), lax.axis_index("c")
    rows_all, slice_width = image_features.shape
    width = image_proj.shape[1]
    half, quarter = rows_all // 2, rows_all // 4
    scale = jnp.exp(log_scale)

    features = {"text": text_features, "image": image_features}
    weights = {"text": text_proj, "image": image_proj}
    towers = ("text", "image")

    halves = {t: half_pair(features[t], c) for t in towers}
    away = jnp.stack(
        [jnp.dot(halves[t][1], weights[t], preferred_element_type=f32).astype(bf16) for t in towers]
    )
    came = swapped(away, "c").astype(f32)
    needed_there, needed_here = {}, {}
    for number, t in enumerate(towers):
        own_sum = jnp.dot(halves[t][0], weights[t], preferred_element_type=f32)
        pair_sum = (own_sum + came[number]).astype(bf16)
        needed_there[t] = lax.dynamic_slice_in_dim(pair_sum, (1 - yh) * quarter, quarter, 0)
        needed_here[t] = lax.dynamic_slice_in_dim(pair_sum, yh * quarter, quarter, 0)

    def normalize(raw):
        inverse = lax.rsqrt(jnp.sum(raw * raw, axis=-1, keepdims=True) + epsilon)
        return raw * inverse, inverse

    own_unit, own_inverse, held = {}, {}, {}
    for t in towers:
        own_raw = needed_here[t].astype(f32) + swapped(needed_there[t], "yh").astype(f32)
        own_unit[t], own_inverse[t] = normalize(own_raw)
        held[t] = own_unit[t].astype(bf16)

    sign = {"text": 1, "image": -1}
    near = {
        t: [from_ahead(held[t], sign[t] * distance) for distance in (2, 3, 1)] for t in towers
    }
    to_complete, _ = lax.optimization_barrier(
        (jnp.stack([needed_here[t] for t in towers]), [near[t][0] for t in towers])
    )
    held = {t: jnp.concatenate([held[t], *near[t]], axis=0) for t in towers}
    completing = swapped(to_complete, "yh").astype(f32)
    held = {t: (held[t], from_ahead(held[t], sign[t] * 4)) for t in towers}

    def in_order(own, other):
        first = jnp.where(yh == 0, own, other)
        second = jnp.where(yh == 0, other, own)
        return jnp.concatenate([first, second], axis=0)

    unit, inverse, gathered_from = {}, {}, {}
    for number, t in enumerate(towers):
        other_raw = needed_there[t].astype(f32) + completing[number]
        other_unit, other_inverse = normalize(other_raw)
        unit[t] = in_order(own_unit[t], other_unit)
        inverse[t] = in_order(own_inverse[t], other_inverse)
        gathered_from[t] = unit[t].astype(bf16)

    place = jnp.stack([c, yh]).astype(jnp.int32)
    numbers = jnp.stack([scale, logit_bias])
    opposite = {"text": "image", "image": "text"}
    sums, away, got, grads = {}, {}, {}, {}
    for t in ("image", "text"):
        if t == "text":
            gathered_from[t], _ = lax.optimization_barrier((gathered_from[t], sums["image"][1]))
        rows = lax.all_gather(gathered_from[t], "c", axis=0, tiled=True)
        mine, other = directions(place, numbers, rows, held[opposite[t]])
        sums[t] = mine, swapped(other, "c")
        away[t] = (mine + sums[t][1].astype(f32)).astype(bf16)
        if t == "text":
            away[t], _ = lax.optimization_barrier((away[t], got["image"]))
        got[t] = swapped(away[t], "yh")
    for t in ("image", "text"):
        tangents = tangent(*sums[t], got[t], unit[t], inverse[t])
        tangent_all = lax.all_gather(tangents, "c", axis=0, tiled=True)
        grads[t] = jnp.einsum("rd,rp->dp", features[t], tangent_all, preferred_element_type=f32)
    grads["image"], _ = lax.optimization_barrier((grads["image"].astype(bf16), away["text"]))
    parts = [scattered_over_x(grads[t]) for t in ("image", "text")]
    image_total, text_total = summed_over_the_rest(jnp.concatenate(parts, axis=0))
    return image_total, text_total


def solution(mesh):
    dp = mesh.shape["dp"]
    fine = Mesh(
        mesh.devices.reshape(dp // (X * YL), X, YL, YH, C), ("z", "x", "yl", "yh", "c")
    )
    head = ("yh", "c")
    placed = (P(DP, head), P(DP, head), P(head, None), P(head, None), P(), P())
    return jax.shard_map(
        per_device,
        mesh=fine,
        in_specs=placed,
        out_specs=(P(head, None), P(head, None)),
        check_vma=False,
    )
```

```python
import jax
import jax.numpy as jnp
from jax import lax
from jax.experimental import pallas as pl
from jax.experimental.pallas import tpu as pltpu
from jax.sharding import Mesh, PartitionSpec as P

STEPS = 8
X, YL, YH, C = 4, 4, 2, 2
LANES = 128
DP = ("z", "x", "yl")

epsilon = 1e-06
bf16 = jnp.bfloat16
f32 = jnp.float32


def from_ahead(block, distance):
    count = lax.axis_size(DP)
    return lax.ppermute(block, DP, [((i + distance) % count, i) for i in range(count)])


def swapped(block, axis):
    return lax.ppermute(block, axis, [(0, 1), (1, 0)])


def spread(block, axis):
    count = lax.axis_size(axis)
    return lax.all_to_all(
        jnp.broadcast_to(block[None], (count,) + block.shape), axis, 0, 0, tiled=True
    )


def half_pair(array, c):
    half = array.shape[-2] // 2
    mine = lax.dynamic_slice_in_dim(array, c * half, half, array.ndim - 2)
    other = lax.dynamic_slice_in_dim(array, (1 - c) * half, half, array.ndim - 2)
    return mine, other


VMEM = pl.BlockSpec(memory_space=pltpu.VMEM)
SMEM = pl.BlockSpec(memory_space=pltpu.SMEM)
VMEM_LIMIT = 32 * 2**20


def directions_kernel(place, numbers, rows_ref, first_ref, second_ref, mine_ref, other_ref):
    c, yh = place[0], place[1]
    scale, bias = numbers[0], numbers[1]
    half = mine_ref.shape[0]
    quarter = half // 2
    for kept in (False, True):
        start = pl.multiple_of((c if kept else 1 - c) * half, half)
        rows = rows_ref[pl.ds(start, half), :]
        total = None
        for block_ref in (first_ref, second_ref):
            block = block_ref[...]
            logits = (
                scale
                * lax.dot_general(
                    rows, block, (((1,), (1,)), ((), ())), preferred_element_type=f32
                )
                + bias
            )
            if kept and block_ref is first_ref:
                row = lax.broadcasted_iota(jnp.int32, logits.shape, 0)
                col = lax.broadcasted_iota(jnp.int32, logits.shape, 1)
                matched = (col < quarter) & (row == col + yh * quarter)
                value = jax.nn.sigmoid(jnp.where(matched, -logits, logits))
                pair_weights = jnp.where(matched, -value, value)
            else:
                pair_weights = jax.nn.sigmoid(logits)
            part = jnp.dot(pair_weights.astype(bf16), block, preferred_element_type=f32)
            total = part if total is None else total + part
        if kept:
            mine_ref[...] = scale * total
        else:
            other_ref[...] = (scale * total).astype(bf16)


def directions(place, numbers, rows, blocks):
    count, width = rows.shape
    half = count // 2
    pairs = count * sum(block.shape[0] for block in blocks)
    return pl.pallas_call(
        directions_kernel,
        out_shape=(
            jax.ShapeDtypeStruct((half, width), f32),
            jax.ShapeDtypeStruct((half, width), bf16),
        ),
        in_specs=[SMEM, SMEM, VMEM, VMEM, VMEM],
        out_specs=(VMEM, VMEM),
        compiler_params=pltpu.CompilerParams(vmem_limit_bytes=VMEM_LIMIT),
        cost_estimate=pl.CostEstimate(
            flops=4 * pairs * width, bytes_accessed=10 * count * width, transcendentals=pairs
        ),
    )(place, numbers, rows, *blocks)


def tangent_kernel(mine_ref, came_ref, got_ref, unit_ref, inverse_ref, out_ref):
    unit = unit_ref[...]
    direction = mine_ref[...] + came_ref[...].astype(f32) + got_ref[...].astype(f32)
    along = jnp.sum(unit * direction, axis=-1, keepdims=True)
    out_ref[...] = ((direction - unit * along) * inverse_ref[...]).astype(bf16)


def tangent(mine, came, got, unit, inverse):
    return pl.pallas_call(
        tangent_kernel,
        out_shape=jax.ShapeDtypeStruct(mine.shape, bf16),
        in_specs=[VMEM] * 5,
        out_specs=VMEM,
        compiler_params=pltpu.CompilerParams(vmem_limit_bytes=VMEM_LIMIT),
        cost_estimate=pl.CostEstimate(
            flops=8 * mine.size, bytes_accessed=14 * mine.size, transcendentals=0
        ),
    )(mine, came, got, unit, inverse)


def lanes_first(rows):
    return rows.reshape(rows.shape[0], -1, LANES).swapaxes(0, 1)


def scattered_over_x(grad):
    got = lax.all_to_all(
        grad.astype(bf16).reshape(X, -1, grad.shape[1]), "x", 0, 0, tiled=True
    )
    return jnp.sum(got.astype(f32), axis=0).astype(bf16)


def summed_over_the_rest(part):
    part = lanes_first(part)
    tiles, height, _ = part.shape
    across = ("z", "yl")
    count = lax.axis_size(across)
    piece = -(-tiles * height // (8 * count)) * 8
    flat = jnp.pad(part.reshape(-1, LANES), ((0, count * piece - tiles * height), (0, 0)))
    got = lax.all_to_all(flat.reshape(count, piece, LANES), across, 0, 0, tiled=True)
    part = jnp.sum(got.astype(f32), axis=0).astype(bf16)
    part = spread(part, across).reshape(-1, LANES)[: tiles * height]
    part = part.reshape(tiles, height, LANES).swapaxes(0, 1).reshape(height, tiles * LANES)
    total = spread(part, "x").reshape(X, 2, height // 2, -1).astype(f32)
    return [total[:, tower].reshape(X * height // 2, -1) for tower in range(2)]


def per_device(image_features, text_features, image_proj, text_proj, log_scale, logit_bias):
    yh, c = lax.axis_index("yh"), lax.axis_index("c")
    rows_all, slice_width = image_features.shape
    width = image_proj.shape[1]
    half, quarter = rows_all // 2, rows_all // 4
    scale = jnp.exp(log_scale)

    features = {"text": text_features, "image": image_features}
    weights = {"text": text_proj, "image": image_proj}
    towers = ("text", "image")

    halves = {t: half_pair(features[t], c) for t in towers}
    away = jnp.stack(
        [jnp.dot(halves[t][1], weights[t], preferred_element_type=f32).astype(bf16) for t in towers]
    )
    came = swapped(away, "c").astype(f32)
    needed_there, needed_here = {}, {}
    for number, t in enumerate(towers):
        own_sum = jnp.dot(halves[t][0], weights[t], preferred_element_type=f32)
        pair_sum = (own_sum + came[number]).astype(bf16)
        needed_there[t] = lax.dynamic_slice_in_dim(pair_sum, (1 - yh) * quarter, quarter, 0)
        needed_here[t] = lax.dynamic_slice_in_dim(pair_sum, yh * quarter, quarter, 0)

    def normalize(raw):
        inverse = lax.rsqrt(jnp.sum(raw * raw, axis=-1, keepdims=True) + epsilon)
        return raw * inverse, inverse

    own_unit, own_inverse, held = {}, {}, {}
    for t in towers:
        own_raw = needed_here[t].astype(f32) + swapped(needed_there[t], "yh").astype(f32)
        own_unit[t], own_inverse[t] = normalize(own_raw)
        held[t] = own_unit[t].astype(bf16)

    sign = {"text": 1, "image": -1}
    near = {
        t: [from_ahead(held[t], sign[t] * distance) for distance in (2, 3, 1)] for t in towers
    }
    to_complete, _ = lax.optimization_barrier(
        (jnp.stack([needed_here[t] for t in towers]), [near["text"][0], held["image"]])
    )
    held = {t: jnp.concatenate([held[t], *near[t]], axis=0) for t in towers}
    completing = swapped(to_complete, "yh").astype(f32)
    held = {t: (held[t], from_ahead(held[t], sign[t] * 4)) for t in towers}

    def in_order(own, other):
        first = jnp.where(yh == 0, own, other)
        second = jnp.where(yh == 0, other, own)
        return jnp.concatenate([first, second], axis=0)

    unit, inverse, gathered_from = {}, {}, {}
    for number, t in enumerate(towers):
        other_raw = needed_there[t].astype(f32) + completing[number]
        other_unit, other_inverse = normalize(other_raw)
        unit[t] = in_order(own_unit[t], other_unit)
        inverse[t] = in_order(own_inverse[t], other_inverse)
        gathered_from[t] = unit[t].astype(bf16)

    place = jnp.stack([c, yh]).astype(jnp.int32)
    numbers = jnp.stack([scale, logit_bias])
    opposite = {"text": "image", "image": "text"}
    sums, away, got, grads = {}, {}, {}, {}
    for t in ("image", "text"):
        if t == "text":
            gathered_from[t], _ = lax.optimization_barrier((gathered_from[t], sums["image"][1]))
        rows = lax.all_gather(gathered_from[t], "c", axis=0, tiled=True)
        mine, other = directions(place, numbers, rows, held[opposite[t]])
        sums[t] = mine, swapped(other, "c")
        away[t] = (mine + sums[t][1].astype(f32)).astype(bf16)
        if t == "text":
            away[t], _ = lax.optimization_barrier((away[t], got["image"]))
        got[t] = swapped(away[t], "yh")
    for t in ("image", "text"):
        tangents = tangent(*sums[t], got[t], unit[t], inverse[t])
        tangent_all = lax.all_gather(tangents, "c", axis=0, tiled=True)
        grads[t] = jnp.einsum("rd,rp->dp", features[t], tangent_all, preferred_element_type=f32)
    grads["image"], _ = lax.optimization_barrier((grads["image"].astype(bf16), away["text"]))
    parts = [scattered_over_x(grads[t]) for t in ("image", "text")]
    image_total, text_total = summed_over_the_rest(jnp.concatenate(parts, axis=0))
    return image_total, text_total


def solution(mesh):
    dp = mesh.shape["dp"]
    fine = Mesh(
        mesh.devices.reshape(dp // (X * YL), X, YL, YH, C), ("z", "x", "yl", "yh", "c")
    )
    head = ("yh", "c")
    placed = (P(DP, head), P(DP, head), P(head, None), P(head, None), P(), P())
    return jax.shard_map(
        per_device,
        mesh=fine,
        in_specs=placed,
        out_specs=(P(head, None), P(head, None)),
        check_vma=False,
    )
```
